128 devices in a mesh: grp: 4 (over x_hi, core), blk: 32 (over x_lo, y, z).
Axes of the slice: x: 4 (x_hi: 2, x_lo: 2; x = x_hi * 2 + x_lo), y: 4, z: 4, core: 2. Of those that a mesh axis runs over, the one named last changes fastest.
Arguments:
- queries: bfloat16 [4, 4096, 4096], P('grp', 'blk'), may hold values from -8 to 8
- keys: bfloat16 [4, 4096, 1024], P('grp', 'blk'), may hold values from -6 to 6
- values: bfloat16 [4, 4096, 1024], P('grp', 'blk'), may hold values from -24 to 24
- cache_k: bfloat16 [4, 32, 2, 128, 1024], P('grp', 'blk'), may hold values from -8 to 8
- cache_v: bfloat16 [4, 32, 2, 128, 1024], P('grp', 'blk'), may hold values from -24 to 24
- holder: int32 [32, 4, 1], replicated, may hold values from 0 to 3; in each aligned block of 4 rows (0 to 3, 4 to 7, ..., all dimensions but the last counted through in order) at most 2 rows name the same one
- prefix_len: int32 [4], replicated, may hold values from 1 to 32, 80 in all
Outputs:
- attended: bfloat16 [4, 4096, 4096], P('grp', 'blk')
The draws below stay inside these ranges and needn't reach their ends.
Inputs may be any that keep to these rules, and one draw needn't show every extreme that they name: Within one column holder[b, :, 0] no index of grp is named more than 2 times, and in some column one is named exactly 2 times. `prefix_len`: some stretch has all 32 blocks.
All inputs are finite; a program needn't handle non-finite values.
Results may differ from the reference program's by a relative error of at most 0.017.
Values may be sent and summed in bfloat16 or wider, within the bound.
A program may use at most 128 MiB of HBM per device.

```python
import math
import jax
import jax.numpy as jnp
import numpy as np
from jax import lax

KV_HEADS = 8
HEAD_DIM = 128
PB_DEV = 1
BLOCK = 128
GROUP = 4
STRETCHES = 4
STRETCH_LEN = 4096
PBLK = 32
SLOTS = 2
KVW = 1024
QW = 4096
N_BLK = 32


def draw_queries(key, part):
    key = jax.random.fold_in(key, 11)
    array_shape = (STRETCHES, STRETCH_LEN, QW)
    drawn = jnp.clip(jax.random.normal(key, array_shape, jnp.float32), -6.0, 6.0)
    return drawn.astype(jnp.bfloat16)


def draw_cache_k(key, part):
    key = jax.random.fold_in(key, 12)
    array_shape = (STRETCHES, N_BLK, SLOTS, BLOCK, KVW)
    drawn = jnp.clip(jax.random.normal(key, array_shape, jnp.float32), -6.0, 6.0)
    return drawn.astype(jnp.bfloat16)


def block_scale(own_key, dims, split, smallest, largest):
    factor_of, own = 1.0, jax.random.fold_in(own_key, 6)
    for axis_at, blocks in split:
        draws = jnp.exp(jax.random.uniform(jax.random.fold_in(own, axis_at), (blocks,), jnp.float32, smallest / len(split), largest / len(split)))
        factor_of = factor_of * jnp.repeat(draws, dims[axis_at] // blocks).reshape([-1 if axis == axis_at else 1 for axis in range(len(dims))])
    return factor_of


def length_profile(number_of, total, most, lean):
    loads = [(1 << 20) // math.isqrt(standing ** lean) + 1 for standing in range(2, number_of + 1)]
    spare, holding = total - most - (number_of - 1), [1] * (number_of - 1)
    while spare > 0:
        movable = [i for i in range(number_of - 1) if holding[i] < most]
        whole, remaining = sum([loads[i] for i in movable]), spare
        for i in movable:
            more = min(most - holding[i], max(1, remaining * loads[i] // whole), spare)
            holding[i] = holding[i] + more
            spare = spare - more
    return np.array([most] + holding)


def uneven(rng, count, total, most, slope):
    if count == 2:
        one = jax.random.randint(rng, (), max(1, total - most), min(most, total - 1) + 1)
        return jnp.stack([one, total - one])
    lengths = jnp.asarray(length_profile(count, total, most, slope), jnp.int32)
    pairs = (count - 1) // 2
    donor, taker = lengths[1:1 + 2 * pairs:2], lengths[2:2 + 2 * pairs:2]
    slack = jnp.minimum(donor - 1, most - taker)
    passed = jax.random.randint(jax.random.fold_in(rng, 1), (pairs,), 0, 1 << 20) % (slack + 1)
    lengths = lengths.at[1:1 + 2 * pairs:2].set(donor - passed).at[2:2 + 2 * pairs:2].set(taker + passed)
    return lengths[jax.random.permutation(jax.random.fold_in(rng, 2), count)]


def assign_block(key, own, number, rows, number_of, top, most, lean):
    order = jax.random.permutation(key, number_of)
    packed, common = shares(number_of, rows * top, most, lean, True), shares(number_of, rows * top, most, lean, False)
    places = jnp.arange(number_of)

    def named(tallies, turn):
        used = int((tallies > 0).sum())
        fixed = max(1, used // 4)
        shifted = fixed + (places - fixed + turn * (used - fixed)) % max(1, number_of - fixed)
        return jnp.zeros((number_of,), jnp.int32).at[order[jnp.where(places < fixed, places, shifted)]].set(jnp.asarray(tallies, jnp.int32))

    tallies = jnp.where(number % 4 == 0, named(packed, number // 4), named(common, number - number // 4 - 1))
    mixed = jax.random.permutation(jax.random.fold_in(own, 3), number_of)
    source_of, sink = mixed[0:number_of // 2 * 2:2], mixed[1:number_of // 2 * 2:2]
    margin = jnp.minimum(tallies[source_of] - 1, most - tallies[sink]) // 2
    margin = jnp.where((source_of == order[0]) | (sink == order[0]) | (tallies[sink] == 0), 0, jnp.maximum(margin, 0))
    shifted = jax.random.randint(jax.random.fold_in(own, 4), (number_of // 2,), 0, 1 << 20) % (margin + 1)
    tallies = tallies.at[source_of].add(-shifted).at[sink].add(shifted)
    labels = jnp.searchsorted(jnp.cumsum(tallies), jnp.arange(rows * top), side="right").astype(jnp.int32)
    grid = labels.reshape(top, rows).T
    grid = grid[jax.random.permutation(jax.random.fold_in(own, 1), rows)]
    turn = jax.random.randint(jax.random.fold_in(own, 2), (rows, 1), 0, top)
    return jnp.take_along_axis(grid, (jnp.arange(top)[None, :] + turn) % top, axis=1)


def shares(count, total, most, lean, full):
    portions = [(1 << 20) // math.isqrt(rank ** lean) + 1 for rank in range(1, count + 1)]
    largest = most if full else min(most, max(-(-total // count), total * portions[0] // sum(portions)))
    least = 1 if total - largest >= count - 1 else 0
    counts, spare = [largest] + [least] * (count - 1), total - largest - least * (count - 1)
    while spare > 0:
        movable = [i for i in range(1, count) if counts[i] < largest] or [i for i in range(1, count) if counts[i] < most]
        pool, left = sum([portions[i] for i in movable]), spare
        for i in movable:
            addition = min(most - counts[i], max(1, left * portions[i] // pool), spare)
            counts[i] = counts[i] + addition
            spare = spare - addition
    return np.array(counts)


def scatter_about(stream_key, extent, spread, bound, shards=(), held_as=jnp.bfloat16):
    values = spread * jax.random.normal(stream_key, extent, jnp.float32)
    if shards:
        values = values * block_scale(stream_key, extent, shards, -0.22, 0.18)
    return jnp.clip(values, -bound, bound).astype(held_as)


def setup_inputs(seed: int = 0) -> dict:
    streams_of = jax.random.split(jax.random.key(seed), 8)
    queries = draw_queries(jax.random.fold_in(streams_of[7], 71), 0)
    keys = scatter_about(streams_of[1], (STRETCHES, STRETCH_LEN, KVW), 1.0, 6.0, ((0, 4), (1, 32)))
    values = scatter_about(streams_of[2], (STRETCHES, STRETCH_LEN, KVW), 4.0, 24.0, ((0, 4), (1, 32)))
    cache_k = draw_cache_k(jax.random.fold_in(streams_of[7], 71), 0)
    cache_v = scatter_about(streams_of[4], (STRETCHES, N_BLK, SLOTS, BLOCK, KVW), 4.0, 24.0, ((0, 4), (1, 32)))
    holder_keys = jax.random.split(jax.random.fold_in(streams_of[5], 1), N_BLK * (STRETCHES * PB_DEV) // (STRETCHES * PB_DEV))
    holder_turns = jax.random.permutation(jax.random.fold_in(streams_of[5], 3), N_BLK * (STRETCHES * PB_DEV) // (STRETCHES * PB_DEV))
    holder = jax.vmap(lambda own, number: assign_block(jax.random.fold_in(streams_of[5], 2), own, number, STRETCHES * PB_DEV, STRETCHES, 1, SLOTS, 2))(holder_keys, holder_turns).reshape((N_BLK, STRETCHES * PB_DEV, 1))
    prefix_len = uneven(streams_of[6], STRETCHES, STRETCHES * PBLK * 5 // 8, PBLK, 2).astype(jnp.int32)
    return {"queries": queries, "keys": keys, "values": values, "cache_k": cache_k, "cache_v": cache_v, "holder": holder, "prefix_len": prefix_len}


NEG_FILL = -1e30


def attend_rows(query_rows, key_rows, value_rows, visible):
    scores = jnp.einsum("tgd,ld->tgl", query_rows.astype(jnp.float32), key_rows.astype(jnp.float32)) * (HEAD_DIM ** -0.5)
    live = visible[:, None, :]
    masked = jnp.where(live, scores, NEG_FILL)
    best_score = jnp.max(masked, axis=-1, keepdims=True)
    weights = jnp.where(live, jnp.exp(masked - best_score), 0.0)
    weight_sum = jnp.sum(weights, axis=-1)
    rounded = lax.optimization_barrier(weights.astype(jnp.bfloat16)).astype(jnp.float32)
    weighted = jnp.einsum("tgl,ld->tgd", rounded, value_rows.astype(jnp.float32))
    return weighted / weight_sum[..., None]


def reference(queries, keys, values, cache_k, cache_v, holder, prefix_len):
    column = holder[:, :, 0]
    width = column.shape[1]
    position = jnp.arange(width, dtype=jnp.int32)
    earlier = position[None, :] < position[:, None]
    same_group = column[:, :, None] == column[:, None, :]
    slot_ids = jnp.sum(jnp.logical_and(same_group, earlier[None]).astype(jnp.int32), axis=2)
    block_ids = jnp.broadcast_to(jnp.arange(N_BLK, dtype=jnp.int32)[:, None], column.shape)
    prefix_keys = cache_k[column, block_ids, slot_ids]
    prefix_values = cache_v[column, block_ids, slot_ids]
    prefix_keys = prefix_keys.reshape(N_BLK, STRETCHES, PB_DEV, BLOCK, KVW).transpose(1, 0, 2, 3, 4).reshape(STRETCHES, PBLK * BLOCK, KVW)
    prefix_values = prefix_values.reshape(N_BLK, STRETCHES, PB_DEV, BLOCK, KVW).transpose(1, 0, 2, 3, 4).reshape(STRETCHES, PBLK * BLOCK, KVW)
    query_block = math.gcd(STRETCH_LEN, 512)
    results = []
    for stretch in range(STRETCHES):
        all_keys = jnp.concatenate([prefix_keys[stretch], keys[stretch]], axis=0)
        all_values = jnp.concatenate([prefix_values[stretch], values[stretch]], axis=0)
        limit = prefix_len[stretch] * BLOCK
        prefix_live = jnp.arange(PBLK * BLOCK, dtype=jnp.int32) < limit
        stretch_queries = queries[stretch]

        def one_block(start):
            query_pos = start + jnp.arange(query_block, dtype=jnp.int32)
            stretch_live = jnp.arange(STRETCH_LEN, dtype=jnp.int32)[None, :] <= query_pos[:, None]
            visible = jnp.concatenate([jnp.broadcast_to(prefix_live[None, :], (query_block, PBLK * BLOCK)), stretch_live], axis=1)
            query_rows = lax.dynamic_slice_in_dim(stretch_queries, start, query_block, 0).reshape(query_block, KV_HEADS, GROUP, HEAD_DIM)
            pieces = []
            for head in range(KV_HEADS):
                lower = head * HEAD_DIM
                pieces.append(attend_rows(query_rows[:, head], all_keys[:, lower:lower + HEAD_DIM], all_values[:, lower:lower + HEAD_DIM], visible))
            return jnp.stack(pieces, axis=1).reshape(query_block, QW)

        starts = jnp.arange(STRETCH_LEN // query_block, dtype=jnp.int32) * query_block
        blocks_out = lax.map(one_block, starts).reshape(STRETCH_LEN, QW)
        results.append(blocks_out.astype(jnp.bfloat16))
    return jnp.stack(results)
```

```python
import functools

import jax
import jax.numpy as jnp
from jax import lax
from jax.experimental import pallas as pl
from jax.experimental.pallas import tpu as pltpu
from jax.sharding import PartitionSpec as P

MESH = pl.DeviceIdType.MESH
BF = jnp.bfloat16
F32 = jnp.float32
BIG = 1e30
SCALE = 1.4426950408889634 / (128.0 ** 0.5)


def attend_kernel(
    q_ref, k_ref, v_ref, ck_ref, cv_ref, holder_ref, plen_ref, o_ref,
    kv, q_in, q_hi, q_lo, acc, top, s0, s1, ob,
    skv, sib_out, sib_in, cand, pc, pens,
    s_sib, r_sib, s_st, r_st, s_q, r_q, s_p, r_p, s_z, r_z, s_f, r_f, s_o, r_o,
):
    g = lax.axis_index("grp")
    b = lax.axis_index("blk")
    xh, core = g // 2, g % 2
    h, z = b // 4, b % 4

    def plane(d):
        return (g, ((h + d) % 8) * 4 + z)

    def across(d):
        return ((1 - xh) * 2 + core, ((h + d) % 8) * 4 + z)

    sibling = (xh * 2 + 1 - core, b)
    z_up = (g, h * 4 + (z + 1) % 4)
    z_down = (g, h * 4 + (z + 3) % 4)

    barrier = pltpu.get_barrier_semaphore()
    peers = [plane(d) for d in range(1, 8)] + [across(d) for d in range(8)] + [sibling, z_up, z_down]
    for peer in peers:
        pl.semaphore_signal(barrier, inc=1, device_id=peer, device_id_type=MESH)

    def remote(src, dst, send, recv, peer):
        return pltpu.make_async_remote_copy(
            src_ref=src, dst_ref=dst, send_sem=send, recv_sem=recv, device_id=peer, device_id_type=MESH
        )

    def held(c):
        own = holder_ref[b, c]
        slot = jnp.int32(0)
        for c2 in range(4):
            slot = slot + jnp.where((c2 < c) & (holder_ref[b, c2] == own), 1, 0)
        return own, jnp.minimum(slot, 1)

    for e in range(2):
        _, slot = held(2 * e + 1 - core)
        sib_out[e, 0] = ck_ref[slot]
        sib_out[e, 1] = cv_ref[slot]
    for p in range(8):
        lanes = slice(p * 128, (p + 1) * 128)
        skv[p, 0] = k_ref[:, lanes]
        skv[p, 1] = v_ref[:, lanes].T
    plen = plen_ref[g]
    for c in range(4, 8):
        for n in range(8):
            u, k = n // 4, n % 4
            if c == 4:
                block = 4 * n + z
            elif c == 7:
                block = 4 * n + (z + 2) % 4
            else:
                block = 4 * (4 * (c - 5) + k) + (z + (3 if u == 0 else 1)) % 4
            pens[c, n] = jnp.where(block < plen, 0.0, BIG)
    for c in range(4):
        for n in range(8):
            pens[c, n] = 0.0
    top[...] = jnp.full(top.shape, -BIG, F32)
    acc[...] = jnp.zeros(acc.shape, F32)

    pl.semaphore_wait(barrier, len(peers))

    sib_copy = remote(sib_out, sib_in, s_sib.at[0], r_sib.at[0], sibling)
    sib_copy.start()
    st_copies, q_copies, p_copies = [], [], []
    for d in range(1, 8):
        to = (h + d) % 8
        copy = remote(skv.at[to], kv.at[h // 2, h % 2, 0], s_st.at[d], r_st.at[d], plane(d))
        copy.start()
        st_copies.append(copy)
    for d in range(1, 8):
        to = (h + d) % 8
        lanes = pl.ds(pl.multiple_of(to * 512, 512), 512)
        copy = remote(q_ref.at[:, lanes], q_in.at[h], s_q.at[d], r_q.at[d], plane(d))
        copy.start()
        q_copies.append(copy)
    kv[h // 2, h % 2, 0] = skv[h]
    q_in[h] = q_ref[:, pl.ds(pl.multiple_of(h * 512, 512), 512)]

    sib_copy.wait_recv()
    for e in range(2):
        own, slot = held(2 * e + core)
        from_sibling = own == xh * 2 + 1 - core
        for p in range(8):
            lanes = slice(p * 128, (p + 1) * 128)
            cand[e, p, 0] = jnp.where(from_sibling, sib_in[e, 0, :, lanes], ck_ref[slot, :, lanes])
            cand[e, p, 1] = jnp.where(from_sibling, sib_in[e, 1, :, lanes], cv_ref[slot, :, lanes])
    for d in range(8):
        to = (h + d) % 8
        copy = remote(cand.at[1 - xh, to], pc.at[xh, h], s_p.at[8 + d], r_p.at[8 + d], across(d))
        copy.start()
        p_copies.append(copy)
        if d:
            copy = remote(cand.at[xh, to], pc.at[xh, h], s_p.at[d], r_p.at[d], plane(d))
            copy.start()
            p_copies.append(copy)
    pc[xh, h] = cand[xh, h]

    for copy in st_copies:
        copy.wait_recv()

    def stretch_up(j):
        return remote(kv.at[j, :, 0], kv.at[j, :, 1], s_z.at[j, 0], r_z.at[j, 0], z_up)

    def stretch_down(j):
        return remote(kv.at[j, :, 0], kv.at[j, :, 3], s_z.at[j, 1], r_z.at[j, 1], z_down)

    def stretch_on_up(j):
        return remote(kv.at[j, :, 1, 0], kv.at[j, :, 2, 0], s_f.at[j, 0], r_f.at[j, 0], z_up)

    def stretch_on_down(j):
        return remote(kv.at[j, :, 3, 1], kv.at[j, :, 2, 1], s_f.at[j, 1], r_f.at[j, 1], z_down)

    def prefix_up(u):
        return remote(kv.at[4, u], kv.at[5 + u, 0], s_z.at[4 + u, 0], r_z.at[4 + u, 0], z_up)

    def prefix_down(u):
        return remote(kv.at[4, u], kv.at[5 + u, 1], s_z.at[4 + u, 1], r_z.at[4 + u, 1], z_down)

    def prefix_on_up(u):
        return remote(kv.at[5 + u, 0, :, 0], kv.at[7, u, :, 0], s_f.at[4 + u, 0], r_f.at[4 + u, 0], z_up)

    def prefix_on_down(u):
        return remote(kv.at[5 + u, 1, :, 1], kv.at[7, u, :, 1], s_f.at[4 + u, 1], r_f.at[4 + u, 1], z_down)

    for j in range(4):
        stretch_up(j).start()
        stretch_down(j).start()

    def forward_stretch(j):
        stretch_up(j).wait_recv()
        stretch_on_up(j).start()
        stretch_down(j).wait_recv()
        stretch_on_down(j).start()

    forward_stretch(0)

    def prepare(i, _):
        for m in range(4):
            x = q_in[i, :, m * 128 : (m + 1) * 128].astype(F32) * SCALE
            hi = x.astype(BF)
            rows = slice(m * 128, (m + 1) * 128)
            q_hi[i, rows] = hi
            q_lo[i, rows] = (x - hi.astype(F32)).astype(BF)
        return 0

    for copy in q_copies:
        copy.wait_recv()
    lax.fori_loop(0, 8, prepare, 0)

    def scores(c, i):
        keys = kv[c, :, :, 0].reshape(1024, 128)
        queries = jnp.concatenate([q_hi[i], q_lo[i]], axis=1)
        keys = jnp.concatenate([keys, keys], axis=1)
        return lax.dot_general(keys, queries, (((1,), (1,)), ((), ())), preferred_element_type=F32)

    def soften(s_ref, c, i, blocks, pen, corner=None):
        parts = []
        best = top[i]
        for n in range(blocks):
            part = s_ref[n * 128 : (n + 1) * 128, :]
            if n == corner:
                key_at = lax.broadcasted_iota(jnp.int32, (128, 512), 0)
                query_at = lax.broadcasted_iota(jnp.int32, (128, 512), 1) % 128
                part = jnp.where(key_at <= query_at, part, -BIG)
            parts.append(part)
            high = jnp.max(part, axis=0, keepdims=True)
            if pen[n] is not None:
                high = high - pen[n]
            best = jnp.maximum(best, high)
        fade = jnp.exp2(top[i] - best)
        top[i] = best
        weights = []
        for n in range(blocks):
            base = best if pen[n] is None else best + pen[n]
            weights.append(jnp.exp2(parts[n] - base).astype(BF))
        weights = jnp.concatenate(weights, axis=0)
        values_t = jnp.concatenate([kv[c, n // 4, n % 4, 1] for n in range(blocks)], axis=1)
        values_t = jnp.concatenate([values_t, jnp.ones((16, blocks * 128), BF)], axis=0)
        acc[i] = acc[i] * fade + jnp.dot(values_t, weights, preferred_element_type=F32)

    def pair(c, t, c_next, t_next):
        pen = [pens[c, n] for n in range(8)]
        s1[...] = scores(c, 2 * t + 1)
        soften(s0, c, 2 * t, 8, pen)
        s0[...] = scores(c_next, 2 * t_next)
        soften(s1, c, 2 * t + 1, 8, pen)

    later = [jnp.where(r <= z, 0.0, BIG) for r in range(4)]

    def diagonal(t):
        s1[...] = scores(t, 2 * t + 1)
        soften(s0, t, 2 * t, 4, [None] + later[1:], corner=0)
        soften(s1, t, 2 * t + 1, 8, [None] * 5 + later[1:], corner=4)

    def stretch_run(t, _):
        @pl.when(t < 3)
        def _():
            forward_stretch(t + 1)

        stretch_on_up(t).wait_recv()
        stretch_on_down(t).wait_recv()
        s0[...] = scores(0, 2 * t)

        def inner(j, _):
            pair(j, t, j + 1, t)
            return 0

        lax.fori_loop(0, t, inner, 0)
        diagonal(t)
        return 0

    lax.fori_loop(0, 4, stretch_run, 0)

    for copy in p_copies:
        copy.wait_recv()

    def pick(n, _):
        side = holder_ref[4 * n + z, g] // 2
        kv[4, n // 4, n % 4, 0] = pc[side, n, 0]
        kv[4, n // 4, n % 4, 1] = pc[side, n, 1].T
        return 0

    lax.fori_loop(0, 8, pick, 0)
    for u in range(2):
        prefix_up(u).start()
        prefix_down(u).start()

    def forward_prefix(u):
        prefix_up(u).wait_recv()
        prefix_on_up(u).start()
        prefix_down(u).wait_recv()
        prefix_on_down(u).start()

    def chunk_run(c, _):
        @pl.when(c == 5)
        def _():
            forward_prefix(0)

        s0[...] = scores(c, 0)

        def inner(t, _):
            pair(c, t, c, (t + 1) % 4)
            return 0

        lax.fori_loop(0, 4, inner, 0)
        return 0

    lax.fori_loop(4, 6, chunk_run, 0)
    forward_prefix(1)
    for u in range(2):
        prefix_on_up(u).wait_recv()
        prefix_on_down(u).wait_recv()

    mine = pl.ds(pl.multiple_of(h * 512, 512), 512)

    def out_copy(i):
        return remote(ob.at[i], o_ref.at[:, mine], s_o.at[i], r_o.at[h], (g, i * 4 + z))

    def own_copy(i):
        return pltpu.make_async_copy(ob.at[i], o_ref.at[:, mine], s_o.at[i])

    def finish(i):
        total = acc[i]
        out = total[0:128] / total[128:129]
        for m in range(4):
            lanes = slice(m * 128, (m + 1) * 128)
            ob[i, :, lanes] = out[:, lanes].T.astype(BF)

        @pl.when(i != h)
        def _():
            out_copy(i).start()

        @pl.when(i == h)
        def _():
            own_copy(i).start()

    def last_run(t, _):
        s0[...] = scores(6, 2 * t)

        def inner(c, _):
            pair(c, t, 7, t)
            return 0

        lax.fori_loop(6, 8, inner, 0)
        finish(2 * t)
        finish(2 * t + 1)
        return 0

    lax.fori_loop(0, 4, last_run, 0)

    sib_copy.wait_send()
    for copy in st_copies + q_copies + p_copies:
        copy.wait_send()
    for j in range(4):
        for copy in (stretch_up(j), stretch_down(j), stretch_on_up(j), stretch_on_down(j)):
            copy.wait_send()
    for u in range(2):
        for copy in (prefix_up(u), prefix_down(u), prefix_on_up(u), prefix_on_down(u)):
            copy.wait_send()

    def settle(i, _):
        @pl.when(i != h)
        def _():
            out_copy(i).wait_send()
            lanes = pl.ds(pl.multiple_of(i * 512, 512), 512)
            remote(ob.at[i], o_ref.at[:, lanes], s_o.at[i], r_o.at[i], (g, i * 4 + z)).wait_recv()

        @pl.when(i == h)
        def _():
            own_copy(i).wait()

        return 0

    lax.fori_loop(0, 8, settle, 0)


def local(queries, keys, values, cache_k, cache_v, holder, prefix_len):
    vmem = pl.BlockSpec(memory_space=pltpu.VMEM)
    smem = pl.BlockSpec(memory_space=pltpu.SMEM)
    dma = pltpu.SemaphoreType.DMA
    out = pl.pallas_call(
        attend_kernel,
        out_shape=jax.ShapeDtypeStruct((128, 4096), BF),
        in_specs=[vmem, vmem, vmem, vmem, vmem, smem, smem],
        out_specs=pl.BlockSpec(memory_space=pl.ANY),
        scratch_shapes=[
            pltpu.VMEM((8, 2, 4, 2, 128, 128), BF),
            pltpu.VMEM((8, 128, 512), BF),
            pltpu.VMEM((8, 512, 128), BF),
            pltpu.VMEM((8, 512, 128), BF),
            pltpu.VMEM((8, 144, 512), F32),
            pltpu.VMEM((8, 1, 512), F32),
            pltpu.VMEM((1024, 512), F32),
            pltpu.VMEM((1024, 512), F32),
            pltpu.VMEM((8, 128, 512), BF),
            pltpu.VMEM((8, 2, 128, 128), BF),
            pltpu.VMEM((2, 2, 128, 1024), BF),
            pltpu.VMEM((2, 2, 128, 1024), BF),
            pltpu.VMEM((2, 8, 2, 128, 128), BF),
            pltpu.VMEM((2, 8, 2, 128, 128), BF),
            pltpu.SMEM((8, 8), F32),
            dma((1,)), dma((1,)),
            dma((8,)), dma((8,)),
            dma((8,)), dma((8,)),
            dma((16,)), dma((16,)),
            dma((6, 2)), dma((6, 2)),
            dma((6, 2)), dma((6, 2)),
            dma((8,)), dma((8,)),
        ],
        compiler_params=pltpu.CompilerParams(
            collective_id=0, has_side_effects=True, vmem_limit_bytes=56 * 2**20
        ),
        cost_estimate=pl.CostEstimate(flops=14 * 10**9, bytes_accessed=4 * 2**20, transcendentals=27 * 10**6),
        name="attend",
    )(
        queries[0], keys[0], values[0], cache_k[0, 0], cache_v[0, 0], holder[:, :, 0], prefix_len,
    )
    return out[None]


def solution(mesh):
    return jax.shard_map(
        local,
        mesh=mesh,
        in_specs=(
            P("grp", "blk", None),
            P("grp", "blk", None),
            P("grp", "blk", None),
            P("grp", "blk", None, None, None),
            P("grp", "blk", None, None, None),
            P(),
            P(),
        ),
        out_specs=P("grp", "blk", None),
        check_vma=False,
    )
```

```python
import functools

import jax
import jax.numpy as jnp
from jax import lax
from jax.experimental import pallas as pl
from jax.experimental.pallas import tpu as pltpu
from jax.sharding import PartitionSpec as P

MESH = pl.DeviceIdType.MESH
BF = jnp.bfloat16
F32 = jnp.float32
BIG = 1e30
SCALE = 1.4426950408889634 / (128.0 ** 0.5)
ORDER = (4, 1, 3, 5, 7, 6, 2)


def attend_kernel(
    q_ref, k_ref, v_ref, ck_ref, cv_ref, holder_ref, plen_ref, o_ref,
    kv, q_in, acc, top, s0, s1, ob,
    skv, sib_out, sib_in, cand, pc_k, pc_v, pens,
    s_sib, r_sib, s_st, r_st, s_q, r_q, s_p, r_p, s_z, r_z, s_f, r_f, s_o, r_o,
):
    g = lax.axis_index("grp")
    b = lax.axis_index("blk")
    xh, core = g // 2, g % 2
    h, z = b // 4, b % 4

    def turned(d):
        return ((h // 4 + d // 4) % 2) * 4 + (h % 4 + d % 4) % 4

    def plane(d):
        return (g, turned(d) * 4 + z)

    def across(d):
        return ((1 - xh) * 2 + core, turned(d) * 4 + z)

    sibling = (xh * 2 + 1 - core, b)
    z_up = (g, h * 4 + (z + 1) % 4)
    z_down = (g, h * 4 + (z + 3) % 4)

    barrier = pltpu.get_barrier_semaphore()
    peers = [plane(d) for d in range(1, 8)] + [across(d) for d in range(8)] + [sibling, z_up, z_down]
    for peer in peers:
        pl.semaphore_signal(barrier, inc=1, device_id=peer, device_id_type=MESH)

    def remote(src, dst, send, recv, peer):
        return pltpu.make_async_remote_copy(
            src_ref=src, dst_ref=dst, send_sem=send, recv_sem=recv, device_id=peer, device_id_type=MESH
        )

    def held(c):
        own = holder_ref[b, c]
        slot = jnp.int32(0)
        for c2 in range(4):
            slot = slot + jnp.where((c2 < c) & (holder_ref[b, c2] == own), 1, 0)
        return own, jnp.minimum(slot, 1)

    for e in range(2):
        _, slot = held(2 * e + 1 - core)
        sib_out[e, 0] = ck_ref[slot]
        sib_out[e, 1] = cv_ref[slot]
    for p in range(8):
        lanes = slice(p * 128, (p + 1) * 128)
        skv[p, 0] = k_ref[:, lanes]
        skv[p, 1] = v_ref[:, lanes].T
    plen = plen_ref[g]
    for c in range(4, 8):
        for n in range(8):
            block = 4 * n + (z + (0, 3, 1, 2)[c - 4]) % 4
            pens[c, n] = jnp.where(block < plen, 0.0, BIG)
    for c in range(4):
        for n in range(8):
            pens[c, n] = 0.0
    top[...] = jnp.full(top.shape, -BIG, F32)
    acc[...] = jnp.zeros(acc.shape, F32)

    pl.semaphore_wait(barrier, len(peers))

    sib_copy = remote(sib_out, sib_in, s_sib.at[0], r_sib.at[0], sibling)
    sib_copy.start()
    st_copies, q_copies, p_copies = [], [], ([], [])
    for d in ORDER:
        to = turned(d)
        copy = remote(skv.at[to], kv.at[h // 2, h % 2, 0], s_st.at[d], r_st.at[d], plane(d))
        copy.start()
        st_copies.append(copy)
    for d in ORDER:
        to = turned(d)
        lanes = pl.ds(pl.multiple_of(to * 512, 512), 512)
        copy = remote(q_ref.at[:, lanes], q_in.at[h], s_q.at[d], r_q.at[d], plane(d))
        copy.start()
        q_copies.append(copy)
    kv[h // 2, h % 2, 0] = skv[h]
    q_in[h] = q_ref[:, pl.ds(pl.multiple_of(h * 512, 512), 512)]

    sib_copy.wait_recv()
    for n, cache in ((0, ck_ref), (1, cv_ref)):
        for e in range(2):
            own, slot = held(2 * e + core)
            from_sibling = own == xh * 2 + 1 - core
            for p in range(8):
                lanes = slice(p * 128, (p + 1) * 128)
                cand[n, e, p] = jnp.where(from_sibling, sib_in[e, n, :, lanes], cache[slot, :, lanes])
        for d in (0,) + ORDER:
            to = turned(d)
            copy = remote(cand.at[n, 1 - xh, to], (pc_k, pc_v)[n].at[xh, h], s_p.at[n, 8 + d], r_p.at[n, 8 + d], across(d))
            copy.start()
            p_copies[n].append(copy)
            if d:
                copy = remote(cand.at[n, xh, to], (pc_k, pc_v)[n].at[xh, h], s_p.at[n, d], r_p.at[n, d], plane(d))
                copy.start()
                p_copies[n].append(copy)
        (pc_k, pc_v)[n][xh, h] = cand[n, xh, h]

    for copy in st_copies:
        copy.wait_recv()

    def stretch_up(j):
        return remote(kv.at[j, :, 0], kv.at[j, :, 1], s_z.at[j, 0], r_z.at[j, 0], z_up)

    def stretch_down(j):
        return remote(kv.at[j, :, 0], kv.at[j, :, 3], s_z.at[j, 1], r_z.at[j, 1], z_down)

    def stretch_on_up(j):
        return remote(kv.at[j, :, 1, 0], kv.at[j, :, 2, 0], s_f.at[j, 0], r_f.at[j, 0], z_up)

    def stretch_on_down(j):
        return remote(kv.at[j, :, 3, 1], kv.at[j, :, 2, 1], s_f.at[j, 1], r_f.at[j, 1], z_down)

    def prefix_up(n):
        return remote(kv.at[4, :, :, n], kv.at[5, :, :, n], s_z.at[4 + n, 0], r_z.at[4 + n, 0], z_up)

    def prefix_down(n):
        return remote(kv.at[4, :, :, n], kv.at[6, :, :, n], s_z.at[4 + n, 1], r_z.at[4 + n, 1], z_down)

    def prefix_on_up():
        return remote(kv.at[5, :, :, 0], kv.at[7, :, :, 0], s_f.at[4, 0], r_f.at[4, 0], z_up)

    def prefix_on_down():
        return remote(kv.at[6, :, :, 1], kv.at[7, :, :, 1], s_f.at[4, 1], r_f.at[4, 1], z_down)

    def send_stretch(j):
        stretch_up(j).start()
        stretch_down(j).start()

    def forward_stretch(j):
        stretch_up(j).wait_recv()
        stretch_on_up(j).start()
        stretch_down(j).wait_recv()
        stretch_on_down(j).start()

    def pick(n):
        for copy in p_copies[n]:
            copy.wait_recv()
        for i in range(8):
            side = holder_ref[4 * i + z, g] // 2
            part = (pc_k, pc_v)[n][side, i]
            kv[4, i // 4, i % 4, n] = part.T if n else part
        prefix_up(n).start()
        prefix_down(n).start()

    send_stretch(0)
    send_stretch(1)
    for j in range(3):
        forward_stretch(j)
        if j < 2:
            send_stretch(j + 2)

    for copy in q_copies:
        copy.wait_recv()

    def scores(c, i):
        keys = kv[c, :, :, 0].reshape(1024, 128)
        queries = jnp.concatenate([q_in[i, :, m * 128 : (m + 1) * 128] for m in range(4)], axis=0)
        return lax.dot_general(keys, queries, (((1,), (1,)), ((), ())), preferred_element_type=F32)

    def soften(s_ref, c, i, blocks, pen, corner=None):
        parts = []
        best = top[i]
        for n in range(blocks):
            part = s_ref[n * 128 : (n + 1) * 128, :]
            if n == corner:
                key_at = lax.broadcasted_iota(jnp.int32, (128, 512), 0)
                query_at = lax.broadcasted_iota(jnp.int32, (128, 512), 1) % 128
                part = jnp.where(key_at <= query_at, part, -BIG)
            parts.append(part)
            high = jnp.max(part, axis=0, keepdims=True)
            if pen[n] is not None:
                high = high - pen[n]
            best = jnp.maximum(best, high)
        fade = jnp.exp2((top[i] - best) * SCALE)
        top[i] = best
        weights = []
        for n in range(blocks):
            base = best if pen[n] is None else best + pen[n]
            weights.append(jnp.exp2((parts[n] - base) * SCALE).astype(BF))
        weights = jnp.concatenate(weights, axis=0)
        values_t = jnp.concatenate([kv[c, n // 4, n % 4, 1] for n in range(blocks)], axis=1)
        values_t = jnp.concatenate([values_t, jnp.ones((16, blocks * 128), BF)], axis=0)
        acc[i] = acc[i] * fade + jnp.dot(values_t, weights, preferred_element_type=F32)

    def pair(c, t, c_next, t_next):
        pen = [pens[c, n] for n in range(8)]
        s1[...] = scores(c, 2 * t + 1)
        soften(s0, c, 2 * t, 8, pen)
        s0[...] = scores(c_next, 2 * t_next)
        soften(s1, c, 2 * t + 1, 8, pen)

    later = [jnp.where(r <= z, 0.0, BIG) for r in range(4)]

    def diagonal(t):
        s1[...] = scores(t, 2 * t + 1)
        soften(s0, t, 2 * t, 4, [None] + later[1:], corner=0)
        soften(s1, t, 2 * t + 1, 8, [None] * 5 + later[1:], corner=4)

    def stretch_run(t, _):
        stretch_on_up(t).wait_recv()
        stretch_on_down(t).wait_recv()
        s0[...] = scores(0, 2 * t)

        @pl.when(t == 1)
        def _():
            forward_stretch(3)

        def inner(j, _):
            @pl.when((t == 2) & (j == 1))
            def _():
                pick(0)

            @pl.when((t == 3) & (j == 2))
            def _():
                pick(1)

            pair(j, t, j + 1, t)
            return 0

        lax.fori_loop(0, t, inner, 0)
        diagonal(t)
        return 0

    lax.fori_loop(0, 4, stretch_run, 0)

    prefix_up(0).wait_recv()
    prefix_on_up().start()
    prefix_down(0).wait_recv()

    def chunk_run(c, _):
        @pl.when(c == 5)
        def _():
            prefix_down(1).wait_recv()
            prefix_on_down().start()
            prefix_up(1).wait_recv()

        s0[...] = scores(c, 0)

        def inner(t, _):
            pair(c, t, c, (t + 1) % 4)
            return 0

        lax.fori_loop(0, 4, inner, 0)
        return 0

    lax.fori_loop(4, 6, chunk_run, 0)
    prefix_on_up().wait_recv()
    prefix_on_down().wait_recv()

    mine = pl.ds(pl.multiple_of(h * 512, 512), 512)

    def out_copy(i):
        return remote(ob.at[i], o_ref.at[:, mine], s_o.at[i], r_o.at[h], (g, i * 4 + z))

    def own_copy(i):
        return pltpu.make_async_copy(ob.at[i], o_ref.at[:, mine], s_o.at[i])

    def finish(i):
        total = acc[i]
        out = total[0:128] / total[128:129]
        for m in range(4):
            lanes = slice(m * 128, (m + 1) * 128)
            ob[i, :, lanes] = out[:, lanes].T.astype(BF)

        @pl.when(i != h)
        def _():
            out_copy(i).start()

        @pl.when(i == h)
        def _():
            own_copy(i).start()

    def last_run(n, _):
        t = (h // 2 + 1 + n) % 4
        s0[...] = scores(6, 2 * t)

        def inner(c, _):
            pair(c, t, 7, t)
            return 0

        lax.fori_loop(6, 8, inner, 0)
        finish(2 * t)
        finish(2 * t + 1)
        return 0

    lax.fori_loop(0, 4, last_run, 0)

    sib_copy.wait_send()
    for copy in st_copies + q_copies + p_copies[0] + p_copies[1]:
        copy.wait_send()
    for j in range(4):
        for copy in (stretch_up(j), stretch_down(j), stretch_on_up(j), stretch_on_down(j)):
            copy.wait_send()
    for copy in (prefix_up(0), prefix_down(0), prefix_up(1), prefix_down(1), prefix_on_up(), prefix_on_down()):
        copy.wait_send()

    def settle(i, _):
        @pl.when(i != h)
        def _():
            out_copy(i).wait_send()
            lanes = pl.ds(pl.multiple_of(i * 512, 512), 512)
            remote(ob.at[i], o_ref.at[:, lanes], s_o.at[i], r_o.at[i], (g, i * 4 + z)).wait_recv()

        @pl.when(i == h)
        def _():
            own_copy(i).wait()

        return 0

    lax.fori_loop(0, 8, settle, 0)


def local(queries, keys, values, cache_k, cache_v, holder, prefix_len):
    vmem = pl.BlockSpec(memory_space=pltpu.VMEM)
    smem = pl.BlockSpec(memory_space=pltpu.SMEM)
    dma = pltpu.SemaphoreType.DMA
    out = pl.pallas_call(
        attend_kernel,
        out_shape=jax.ShapeDtypeStruct((128, 4096), BF),
        in_specs=[vmem, vmem, vmem, vmem, vmem, smem, smem],
        out_specs=pl.BlockSpec(memory_space=pl.ANY),
        scratch_shapes=[
            pltpu.VMEM((8, 2, 4, 2, 128, 128), BF),
            pltpu.VMEM((8, 128, 512), BF),
            pltpu.VMEM((8, 144, 512), F32),
            pltpu.VMEM((8, 1, 512), F32),
            pltpu.VMEM((1024, 512), F32),
            pltpu.VMEM((1024, 512), F32),
            pltpu.VMEM((8, 128, 512), BF),
            pltpu.VMEM((8, 2, 128, 128), BF),
            pltpu.VMEM((2, 2, 128, 1024), BF),
            pltpu.VMEM((2, 2, 128, 1024), BF),
            pltpu.VMEM((2, 2, 8, 128, 128), BF),
            pltpu.VMEM((2, 8, 128, 128), BF),
            pltpu.VMEM((2, 8, 128, 128), BF),
            pltpu.SMEM((8, 8), F32),
            dma((1,)), dma((1,)),
            dma((8,)), dma((8,)),
            dma((8,)), dma((8,)),
            dma((2, 16)), dma((2, 16)),
            dma((6, 2)), dma((6, 2)),
            dma((6, 2)), dma((6, 2)),
            dma((8,)), dma((8,)),
        ],
        compiler_params=pltpu.CompilerParams(
            collective_id=0, has_side_effects=True, vmem_limit_bytes=56 * 2**20
        ),
        cost_estimate=pl.CostEstimate(flops=14 * 10**9, bytes_accessed=4 * 2**20, transcendentals=27 * 10**6),
        name="attend",
    )(
        queries[0], keys[0], values[0], cache_k[0, 0], cache_v[0, 0], holder[:, :, 0], prefix_len,
    )
    return out[None]


def solution(mesh):
    return jax.shard_map(
        local,
        mesh=mesh,
        in_specs=(
            P("grp", "blk", None),
            P("grp", "blk", None),
            P("grp", "blk", None),
            P("grp", "blk", None, None, None),
            P("grp", "blk", None, None, None),
            P(),
            P(),
        ),
        out_specs=P("grp", "blk", None),
        check_vma=False,
    )
```

```python
import functools

import jax
import jax.numpy as jnp
from jax import lax
from jax.experimental import pallas as pl
from jax.experimental.pallas import tpu as pltpu
from jax.sharding import PartitionSpec as P

MESH = pl.DeviceIdType.MESH
BF = jnp.bfloat16
F32 = jnp.float32
BIG = 1e30
SCALE = 1.4426950408889634 / (128.0 ** 0.5)
ORDER = (4, 1, 3, 5, 7, 6, 2)
LAST = (6, 2, 5, 7, 1, 3, 4, 0)


def attend_kernel(
    q_ref, k_ref, v_ref, ck_ref, cv_ref, holder_ref, plen_ref, o_ref,
    kv, q_in, acc, top, s0, s1, ob,
    skv, sib_out, sib_in, cand, pc_k, pc_v, k_in, v_in, ck_in, cv_in, pens,
    s_in, s_sib, r_sib, s_st, r_st, s_q, r_q, s_p, r_p, s_z, r_z, s_f, r_f, s_zp, r_zp, s_fp, r_fp, s_o, r_o,
):
    g = lax.axis_index("grp")
    b = lax.axis_index("blk")
    xh, core = g // 2, g % 2
    h, z = b // 4, b % 4

    def turned(d):
        return ((h // 4 + d // 4) % 2) * 4 + (h % 4 + d % 4) % 4

    def plane(d):
        return (g, turned(d) * 4 + z)

    def across(d):
        return ((1 - xh) * 2 + core, turned(d) * 4 + z)

    sibling = (xh * 2 + 1 - core, b)
    z_up = (g, h * 4 + (z + 1) % 4)
    z_down = (g, h * 4 + (z + 3) % 4)

    barrier = pltpu.get_barrier_semaphore()
    peers = [plane(d) for d in range(1, 8)] + [across(d) for d in range(8)] + [sibling, z_up, z_down]
    for peer in peers:
        pl.semaphore_signal(barrier, inc=1, device_id=peer, device_id_type=MESH)

    def remote(src, dst, send, recv, peer):
        return pltpu.make_async_remote_copy(
            src_ref=src, dst_ref=dst, send_sem=send, recv_sem=recv, device_id=peer, device_id_type=MESH
        )

    def held(c):
        own = holder_ref[c, b]
        slot = jnp.int32(0)
        for c2 in range(4):
            slot = slot + jnp.where((c2 < c) & (holder_ref[c2, b] == own), 1, 0)
        return own, jnp.minimum(slot, 1)

    fetches = [
        pltpu.make_async_copy(src, dst, s_in.at[n])
        for n, (src, dst) in enumerate(((k_ref, k_in), (v_ref, v_in), (ck_ref, ck_in), (cv_ref, cv_in)))
    ]
    for fetch in fetches:
        fetch.start()
    own_queries = pltpu.make_async_copy(
        q_ref.at[:, pl.ds(pl.multiple_of(h * 512, 512), 512)], q_in.at[h], s_in.at[4]
    )
    own_queries.start()
    fetches[0].wait()
    fetches[1].wait()
    for p in range(8):
        lanes = slice(p * 128, (p + 1) * 128)
        skv[p, 0] = k_in[:, lanes]
        skv[p, 1] = v_in[:, lanes].T

    pl.semaphore_wait(barrier, len(peers))

    st_copies, q_copies, p_copies = [], [], ([], [])
    for d in ORDER:
        to = turned(d)
        copy = remote(skv.at[to], kv.at[h // 2, h % 2, 0], s_st.at[d], r_st.at[d], plane(d))
        copy.start()
        st_copies.append(copy)
    for d in ORDER:
        to = turned(d)
        lanes = pl.ds(pl.multiple_of(to * 512, 512), 512)
        copy = remote(q_ref.at[:, lanes], q_in.at[h], s_q.at[d], r_q.at[d], plane(d))
        copy.start()
        q_copies.append(copy)

    fetches[2].wait()
    fetches[3].wait()
    for e in range(2):
        _, slot = held(2 * e + 1 - core)
        sib_out[e, 0] = ck_in[slot]
        sib_out[e, 1] = cv_in[slot]
    sib_copy = remote(sib_out, sib_in, s_sib.at[0], r_sib.at[0], sibling)
    sib_copy.start()
    kv[h // 2, h % 2, 0] = skv[h]
    plen = plen_ref[g]
    for c in range(4, 8):
        for n in range(8):
            if c in (4, 7):
                block = 4 * n + (z + 2 * (c // 7)) % 4
            else:
                block = 4 * (4 * (c - 5) + n % 4) + (z + 3 - 2 * (n // 4)) % 4
            pens[c, n] = jnp.where(block < plen, 0.0, BIG)
    for c in range(4):
        for n in range(8):
            pens[c, n] = 0.0
    top[...] = jnp.full(top.shape, -BIG, F32)
    acc[...] = jnp.zeros(acc.shape, F32)

    sib_copy.wait_recv()
    for n, cache in ((0, ck_in), (1, cv_in)):
        for e in range(2):
            own, slot = held(2 * e + core)
            from_sibling = own == xh * 2 + 1 - core
            for p in range(8):
                lanes = slice(p * 128, (p + 1) * 128)
                cand[n, e, p] = jnp.where(from_sibling, sib_in[e, n, :, lanes], cache[slot, :, lanes])
        for d in (0,) + ORDER:
            to = turned(d)
            copy = remote(cand.at[n, 1 - xh, to], (pc_k, pc_v)[n].at[xh, h], s_p.at[n, 8 + d], r_p.at[n, 8 + d], across(d))
            copy.start()
            p_copies[n].append(copy)
            if d:
                copy = remote(cand.at[n, xh, to], (pc_k, pc_v)[n].at[xh, h], s_p.at[n, d], r_p.at[n, d], plane(d))
                copy.start()
                p_copies[n].append(copy)
        (pc_k, pc_v)[n][xh, h] = cand[n, xh, h]

    for copy in st_copies:
        copy.wait_recv()

    def stretch_up(j):
        return remote(kv.at[j, :, 0], kv.at[j, :, 1], s_z.at[j, 0], r_z.at[j, 0], z_up)

    def stretch_down(j):
        return remote(kv.at[j, :, 0], kv.at[j, :, 3], s_z.at[j, 1], r_z.at[j, 1], z_down)

    def stretch_on_up(j):
        return remote(kv.at[j, :, 1, 0], kv.at[j, :, 2, 0], s_f.at[j, 0], r_f.at[j, 0], z_up)

    def stretch_on_down(j):
        return remote(kv.at[j, :, 3, 1], kv.at[j, :, 2, 1], s_f.at[j, 1], r_f.at[j, 1], z_down)

    def prefix_up(n, u):
        return remote(kv.at[4, u, :, n], kv.at[5 + u, 0, :, n], s_zp.at[n, u, 0], r_zp.at[n, u, 0], z_up)

    def prefix_down(n, u):
        return remote(kv.at[4, u, :, n], kv.at[5 + u, 1, :, n], s_zp.at[n, u, 1], r_zp.at[n, u, 1], z_down)

    def prefix_on(n, u):
        return remote(kv.at[5 + u, n, :, n], kv.at[7, u, :, n], s_fp.at[n, u], r_fp.at[n, u], (z_up, z_down)[n])

    def forward_prefix(n, u):
        prefix_up(n, u).wait_recv()
        if n == 0:
            prefix_on(n, u).start()
        prefix_down(n, u).wait_recv()
        if n == 1:
            prefix_on(n, u).start()

    def send_stretch(j):
        stretch_up(j).start()
        stretch_down(j).start()

    def forward_stretch(j):
        stretch_up(j).wait_recv()
        stretch_on_up(j).start()
        stretch_down(j).wait_recv()
        stretch_on_down(j).start()

    def pick(n):
        for copy in p_copies[n]:
            copy.wait_recv()
        for i in range(8):
            side = holder_ref[g, 4 * i + z] // 2
            part = (pc_k, pc_v)[n][side, i]
            kv[4, i // 4, i % 4, n] = part.T if n else part
        for u in range(2):
            prefix_up(n, u).start()
            prefix_down(n, u).start()

    send_stretch(0)
    send_stretch(1)
    for j in range(3):
        forward_stretch(j)
        if j < 2:
            send_stretch(j + 2)

    for copy in q_copies:
        copy.wait_recv()
    own_queries.wait()

    def scores(c, i):
        keys = kv[c, :, :, 0].reshape(1024, 128)
        queries = jnp.concatenate([q_in[i, :, m * 128 : (m + 1) * 128] for m in range(4)], axis=0)
        return lax.dot_general(keys, queries, (((1,), (1,)), ((), ())), preferred_element_type=F32)

    def soften(s_ref, c, i, blocks, pen, corner=None):
        parts = []
        best = top[i]
        for n in range(blocks):
            part = s_ref[n * 128 : (n + 1) * 128, :]
            if n == corner:
                key_at = lax.broadcasted_iota(jnp.int32, (128, 512), 0)
                query_at = lax.broadcasted_iota(jnp.int32, (128, 512), 1) % 128
                part = jnp.where(key_at <= query_at, part, -BIG)
            parts.append(part)
            high = jnp.max(part, axis=0, keepdims=True)
            if pen[n] is not None:
                high = high - pen[n]
            best = jnp.maximum(best, high)
        fade = jnp.exp2((top[i] - best) * SCALE)
        top[i] = best
        weights = []
        for n in range(blocks):
            base = best if pen[n] is None else best + pen[n]
            weights.append(jnp.exp2((parts[n] - base) * SCALE).astype(BF))
        weights = jnp.concatenate(weights, axis=0)
        values_t = jnp.concatenate([kv[c, n // 4, n % 4, 1] for n in range(blocks)], axis=1)
        values_t = jnp.concatenate([values_t, jnp.ones((16, blocks * 128), BF)], axis=0)
        acc[i] = acc[i] * fade + jnp.dot(values_t, weights, preferred_element_type=F32)

    def pair(c, a, b, c_next, a_next):
        pen = [pens[c, n] for n in range(8)]
        s1[...] = scores(c, b)
        soften(s0, c, a, 8, pen)
        s0[...] = scores(c_next, a_next)
        soften(s1, c, b, 8, pen)

    later = [jnp.where(r <= z, 0.0, BIG) for r in range(4)]

    def diagonal(t):
        s1[...] = scores(t, 2 * t + 1)
        soften(s0, t, 2 * t, 4, [None] + later[1:], corner=0)
        s0[...] = scores(jnp.where(t == 3, 4, t), (2 * t + 2) % 8)
        soften(s1, t, 2 * t + 1, 8, [None] * 5 + later[1:], corner=4)

    def gathered(j):
        stretch_on_up(j).wait_recv()
        stretch_on_down(j).wait_recv()

    def stretch_run(j, _):
        @pl.when(j == 3)
        def _():
            pick(1)

        diagonal(j)

        def inner(t, _):
            @pl.when((j == 0) & (t == 2))
            def _():
                forward_stretch(3)

            @pl.when((j == 1) & (t == 2))
            def _():
                pick(0)

            @pl.when(t == 3)
            def _():
                gathered(j + 1)

            last = t == 3
            j_next = jnp.where(last, j + 1, j)
            pair(j, 2 * t, 2 * t + 1, j_next, jnp.where(last, 2 * j + 2, 2 * t + 2))
            return 0

        lax.fori_loop(j + 1, 4, inner, 0)
        return 0

    gathered(0)
    s0[...] = scores(0, 0)
    lax.fori_loop(0, 4, stretch_run, 0)

    def last_tile(n):
        step = jnp.int32(LAST[7])
        for m in range(7):
            step = jnp.where(n % 8 == m, LAST[m], step)
        return turned(step)

    def chunk_run(c, _):
        @pl.when(c == 5)
        def _():
            forward_prefix(1, 0)

        def inner(t, _):
            @pl.when((c == 4) & (t == 2))
            def _():
                forward_prefix(0, 0)
                forward_prefix(0, 1)

            @pl.when((c == 5) & (t == 3))
            def _():
                forward_prefix(1, 1)

            last = t == 3
            a_next = jnp.where(last & (c == 5), last_tile(0), (2 * t + 2) % 8)
            pair(c, 2 * t, 2 * t + 1, jnp.where(last, c + 1, c), a_next)
            return 0

        lax.fori_loop(0, 4, inner, 0)
        return 0

    lax.fori_loop(4, 6, chunk_run, 0)
    for n in range(2):
        for u in range(2):
            prefix_on(n, u).wait_recv()

    mine = pl.ds(pl.multiple_of(h * 512, 512), 512)

    def out_copy(i):
        return remote(ob.at[i], o_ref.at[:, mine], s_o.at[i], r_o.at[h], (g, i * 4 + z))

    def own_copy(i):
        return pltpu.make_async_copy(ob.at[i], o_ref.at[:, mine], s_o.at[i])

    def finish(i):
        total = acc[i]
        out = total[0:128] / total[128:129]
        for m in range(4):
            lanes = slice(m * 128, (m + 1) * 128)
            ob[i, :, lanes] = out[:, lanes].T.astype(BF)

        @pl.when(i != h)
        def _():
            out_copy(i).start()

        @pl.when(i == h)
        def _():
            own_copy(i).start()

    def last_run(n, _):
        i = last_tile(n)
        pen = [[pens[c, m] for m in range(8)] for c in (6, 7)]
        s1[...] = scores(7, i)
        soften(s0, 6, i, 8, pen[0])
        s0[...] = scores(6, last_tile(n + 1))
        soften(s1, 7, i, 8, pen[1])
        finish(i)
        return 0

    lax.fori_loop(0, 8, last_run, 0)

    sib_copy.wait_send()
    for copy in st_copies + q_copies + p_copies[0] + p_copies[1]:
        copy.wait_send()
    for j in range(4):
        for copy in (stretch_up(j), stretch_down(j), stretch_on_up(j), stretch_on_down(j)):
            copy.wait_send()
    for n in range(2):
        for u in range(2):
            for copy in (prefix_up(n, u), prefix_down(n, u), prefix_on(n, u)):
                copy.wait_send()

    def settle(i, _):
        @pl.when(i != h)
        def _():
            out_copy(i).wait_send()
            lanes = pl.ds(pl.multiple_of(i * 512, 512), 512)
            remote(ob.at[i], o_ref.at[:, lanes], s_o.at[i], r_o.at[i], (g, i * 4 + z)).wait_recv()

        @pl.when(i == h)
        def _():
            own_copy(i).wait()

        return 0

    lax.fori_loop(0, 8, settle, 0)


def local(queries, keys, values, cache_k, cache_v, holder, prefix_len):
    hbm = pl.BlockSpec(memory_space=pl.ANY)
    smem = pl.BlockSpec(memory_space=pltpu.SMEM)
    dma = pltpu.SemaphoreType.DMA
    out = pl.pallas_call(
        attend_kernel,
        out_shape=jax.ShapeDtypeStruct((128, 4096), BF),
        in_specs=[hbm] * 5 + [smem, smem],
        out_specs=hbm,
        scratch_shapes=[
            pltpu.VMEM((8, 2, 4, 2, 128, 128), BF),
            pltpu.VMEM((8, 128, 512), BF),
            pltpu.VMEM((8, 144, 512), F32),
            pltpu.VMEM((8, 1, 512), F32),
            pltpu.VMEM((1024, 512), F32),
            pltpu.VMEM((1024, 512), F32),
            pltpu.VMEM((8, 128, 512), BF),
            pltpu.VMEM((8, 2, 128, 128), BF),
            pltpu.VMEM((2, 2, 128, 1024), BF),
            pltpu.VMEM((2, 2, 128, 1024), BF),
            pltpu.VMEM((2, 2, 8, 128, 128), BF),
            pltpu.VMEM((2, 8, 128, 128), BF),
            pltpu.VMEM((2, 8, 128, 128), BF),
            pltpu.VMEM((128, 1024), BF),
            pltpu.VMEM((128, 1024), BF),
            pltpu.VMEM((2, 128, 1024), BF),
            pltpu.VMEM((2, 128, 1024), BF),
            pltpu.SMEM((8, 8), F32),
            dma((5,)),
            dma((1,)), dma((1,)),
            dma((8,)), dma((8,)),
            dma((8,)), dma((8,)),
            dma((2, 16)), dma((2, 16)),
            dma((4, 2)), dma((4, 2)),
            dma((4, 2)), dma((4, 2)),
            dma((2, 2, 2)), dma((2, 2, 2)),
            dma((2, 2)), dma((2, 2)),
            dma((8,)), dma((8,)),
        ],
        compiler_params=pltpu.CompilerParams(
            collective_id=0, has_side_effects=True, vmem_limit_bytes=56 * 2**20
        ),
        cost_estimate=pl.CostEstimate(flops=14 * 10**9, bytes_accessed=4 * 2**20, transcendentals=27 * 10**6),
        name="attend",
    )(
        queries[0], keys[0], values[0], cache_k[0, 0], cache_v[0, 0], holder[:, :, 0].T, prefix_len,
    )
    return out[None]


def solution(mesh):
    return jax.shard_map(
        local,
        mesh=mesh,
        in_specs=(
            P("grp", "blk", None),
            P("grp", "blk", None),
            P("grp", "blk", None),
            P("grp", "blk", None, None, None),
            P("grp", "blk", None, None, None),
            P(),
            P(),
        ),
        out_specs=P("grp", "blk", None),
        check_vma=False,
    )
```

```python
import functools

import jax
import jax.numpy as jnp
from jax import lax
from jax.experimental import pallas as pl
from jax.experimental.pallas import tpu as pltpu
from jax.sharding import PartitionSpec as P

MESH = pl.DeviceIdType.MESH
BF = jnp.bfloat16
F32 = jnp.float32
BIG = 1e30
SCALE = 1.4426950408889634 / (128.0 ** 0.5)
ORDER = (4, 1, 3, 5, 7, 6, 2)
LAST = (6, 2, 5, 7, 1, 3, 4, 0)


def attend_kernel(
    q_ref, k_ref, v_ref, ck_ref, cv_ref, holder_ref, plen_ref, o_ref,
    kv, q_in, acc, top, s0, s1, ob,
    skv, sib_out, sib_in, cand, pc_k, pc_v, k_in, v_in, ck_in, cv_in, pens,
    s_in, s_sib, r_sib, s_st, r_st, s_q, r_q, s_p, r_p, s_z, r_z, s_f, r_f, s_zp, r_zp, s_fp, r_fp, s_o, r_o,
):
    g = lax.axis_index("grp")
    b = lax.axis_index("blk")
    xh, core = g // 2, g % 2
    h, z = b // 4, b % 4

    def turned(d):
        return ((h // 4 + d // 4) % 2) * 4 + (h % 4 + d % 4) % 4

    def plane(d):
        return (g, turned(d) * 4 + z)

    def across(d):
        return ((1 - xh) * 2 + core, turned(d) * 4 + z)

    sibling = (xh * 2 + 1 - core, b)
    z_up = (g, h * 4 + (z + 1) % 4)
    z_down = (g, h * 4 + (z + 3) % 4)

    barrier = pltpu.get_barrier_semaphore()
    peers = [plane(d) for d in range(1, 8)] + [across(d) for d in range(8)] + [sibling, z_up, z_down]
    for peer in peers:
        pl.semaphore_signal(barrier, inc=1, device_id=peer, device_id_type=MESH)

    def remote(src, dst, send, recv, peer):
        return pltpu.make_async_remote_copy(
            src_ref=src, dst_ref=dst, send_sem=send, recv_sem=recv, device_id=peer, device_id_type=MESH
        )

    def held(c):
        own = holder_ref[c, b]
        slot = jnp.int32(0)
        for c2 in range(4):
            slot = slot + jnp.where((c2 < c) & (holder_ref[c2, b] == own), 1, 0)
        return own, jnp.minimum(slot, 1)

    fetches = [
        pltpu.make_async_copy(src, dst, s_in.at[n])
        for n, (src, dst) in enumerate(((k_ref, k_in), (v_ref, v_in), (ck_ref, ck_in), (cv_ref, cv_in)))
    ]
    for fetch in fetches:
        fetch.start()
    own_queries = pltpu.make_async_copy(
        q_ref.at[:, pl.ds(pl.multiple_of(h * 512, 512), 512)], q_in.at[h], s_in.at[4]
    )
    own_queries.start()
    fetches[0].wait()
    fetches[1].wait()
    for p in range(8):
        lanes = slice(p * 128, (p + 1) * 128)
        skv[p, 0] = k_in[:, lanes]
        skv[p, 1] = v_in[:, lanes].T

    pl.semaphore_wait(barrier, len(peers))

    st_copies, q_copies, p_copies = [], [], ([], [])
    for d in ORDER:
        to = turned(d)
        copy = remote(skv.at[to], kv.at[h // 2, h % 2, 0], s_st.at[d], r_st.at[d], plane(d))
        copy.start()
        st_copies.append(copy)
    for d in ORDER:
        to = turned(d)
        lanes = pl.ds(pl.multiple_of(to * 512, 512), 512)
        copy = remote(q_ref.at[:, lanes], q_in.at[h], s_q.at[d], r_q.at[d], plane(d))
        copy.start()
        q_copies.append(copy)

    fetches[2].wait()
    fetches[3].wait()
    for e in range(2):
        _, slot = held(2 * e + 1 - core)
        sib_out[e, 0] = ck_in[slot]
        sib_out[e, 1] = cv_in[slot]
    sib_copy = remote(sib_out, sib_in, s_sib.at[0], r_sib.at[0], sibling)
    sib_copy.start()
    kv[h // 2, h % 2, 0] = skv[h]
    plen = plen_ref[g]
    for c in range(4, 8):
        for n in range(8):
            if c in (4, 7):
                block = 4 * n + (z + 2 * (c // 7)) % 4
            else:
                block = 4 * (4 * (c - 5) + n % 4) + (z + 3 - 2 * (n // 4)) % 4
            pens[c, n] = jnp.where(block < plen, 0.0, BIG)
    for c in range(4):
        for n in range(8):
            pens[c, n] = 0.0
    top[...] = jnp.full(top.shape, -BIG, F32)
    acc[...] = jnp.zeros(acc.shape, F32)

    def send_prefix(n, cache):
        for e in range(2):
            own, slot = held(2 * e + core)
            from_sibling = own == xh * 2 + 1 - core
            for p in range(8):
                lanes = slice(p * 128, (p + 1) * 128)
                part = jnp.where(from_sibling, sib_in[e, n, :, lanes], cache[slot, :, lanes])
                cand[n, e, p] = part.T if n else part
        for d in (0,) + ORDER:
            to = turned(d)
            copy = remote(cand.at[n, 1 - xh, to], (pc_k, pc_v)[n].at[xh, h], s_p.at[n, 8 + d], r_p.at[n, 8 + d], across(d))
            copy.start()
            p_copies[n].append(copy)
            if d:
                copy = remote(cand.at[n, xh, to], (pc_k, pc_v)[n].at[xh, h], s_p.at[n, d], r_p.at[n, d], plane(d))
                copy.start()
                p_copies[n].append(copy)
        (pc_k, pc_v)[n][xh, h] = cand[n, xh, h]

    def stretch_up(j):
        return remote(kv.at[j, :, 0], kv.at[j, :, 1], s_z.at[j, 0], r_z.at[j, 0], z_up)

    def stretch_down(j):
        return remote(kv.at[j, :, 0], kv.at[j, :, 3], s_z.at[j, 1], r_z.at[j, 1], z_down)

    def stretch_on_up(j):
        return remote(kv.at[j, :, 1, 0], kv.at[j, :, 2, 0], s_f.at[j, 0], r_f.at[j, 0], z_up)

    def stretch_on_down(j):
        return remote(kv.at[j, :, 3, 1], kv.at[j, :, 2, 1], s_f.at[j, 1], r_f.at[j, 1], z_down)

    def prefix_up(n, u):
        return remote(kv.at[4, u, :, n], kv.at[5 + u, 0, :, n], s_zp.at[n, u, 0], r_zp.at[n, u, 0], z_up)

    def prefix_down(n, u):
        return remote(kv.at[4, u, :, n], kv.at[5 + u, 1, :, n], s_zp.at[n, u, 1], r_zp.at[n, u, 1], z_down)

    def prefix_on(n, u):
        return remote(kv.at[5 + u, u, :, n], kv.at[7, u, :, n], s_fp.at[n, u], r_fp.at[n, u], (z_up, z_down)[u])

    def forward_prefix(n, u):
        here, other = (prefix_up, prefix_down) if u == 0 else (prefix_down, prefix_up)
        here(n, u).wait_recv()
        prefix_on(n, u).start()
        other(n, u).wait_recv()

    def send_stretch(j):
        stretch_up(j).start()
        stretch_down(j).start()

    def forward_stretch(j):
        stretch_up(j).wait_recv()
        stretch_on_up(j).start()
        stretch_down(j).wait_recv()
        stretch_on_down(j).start()

    def pick(n):
        for copy in p_copies[n]:
            copy.wait_recv()
        for i in range(8):
            side = holder_ref[g, 4 * i + z] // 2
            kv[4, i // 4, i % 4, n] = (pc_k, pc_v)[n][side, i]
        for u in range(2):
            prefix_up(n, u).start()
            prefix_down(n, u).start()

    sib_copy.wait_recv()
    send_prefix(0, ck_in)
    for copy in st_copies:
        copy.wait_recv()
    send_stretch(0)
    send_stretch(1)
    send_prefix(1, cv_in)
    for j in range(3):
        forward_stretch(j)
        if j < 2:
            send_stretch(j + 2)

    for copy in q_copies:
        copy.wait_recv()
    own_queries.wait()

    def scores(c, i):
        keys = kv[c, :, :, 0].reshape(1024, 128)
        queries = jnp.concatenate([q_in[i, :, m * 128 : (m + 1) * 128] for m in range(4)], axis=0)
        return lax.dot_general(keys, queries, (((1,), (1,)), ((), ())), preferred_element_type=F32)

    def soften(s_ref, c, i, blocks, pen, corner=None):
        parts = []
        best = top[i]
        for n in range(blocks):
            part = s_ref[n * 128 : (n + 1) * 128, :]
            if n == corner:
                key_at = lax.broadcasted_iota(jnp.int32, (128, 512), 0)
                query_at = lax.broadcasted_iota(jnp.int32, (128, 512), 1) % 128
                part = jnp.where(key_at <= query_at, part, -BIG)
            parts.append(part)
            high = jnp.max(part, axis=0, keepdims=True)
            if pen[n] is not None:
                high = high - pen[n]
            best = jnp.maximum(best, high)
        fade = jnp.exp2((top[i] - best) * SCALE)
        top[i] = best
        weights = []
        for n in range(blocks):
            base = best if pen[n] is None else best + pen[n]
            weights.append(jnp.exp2((parts[n] - base) * SCALE).astype(BF))
        weights = jnp.concatenate(weights, axis=0)
        values_t = jnp.concatenate([kv[c, n // 4, n % 4, 1] for n in range(blocks)], axis=1)
        values_t = jnp.concatenate([values_t, jnp.ones((16, blocks * 128), BF)], axis=0)
        acc[i] = acc[i] * fade + jnp.dot(values_t, weights, preferred_element_type=F32)

    def pair(c, a, b, c_next, a_next):
        pen = [pens[c, n] for n in range(8)]
        s1[...] = scores(c, b)
        soften(s0, c, a, 8, pen)
        s0[...] = scores(c_next, a_next)
        soften(s1, c, b, 8, pen)

    later = [jnp.where(r <= z, 0.0, BIG) for r in range(4)]

    def diagonal(t):
        s1[...] = scores(t, 2 * t + 1)
        soften(s0, t, 2 * t, 4, [None] + later[1:], corner=0)
        s0[...] = scores(jnp.where(t == 3, 4, t), (2 * t + 2) % 8)
        soften(s1, t, 2 * t + 1, 8, [None] * 5 + later[1:], corner=4)

    def gathered(j):
        stretch_on_up(j).wait_recv()
        stretch_on_down(j).wait_recv()

    def stretch_run(j, _):
        @pl.when(j == 3)
        def _():
            pick(1)

        diagonal(j)

        def inner(t, _):
            @pl.when((j == 0) & (t == 2))
            def _():
                forward_stretch(3)

            @pl.when((j == 0) & (t == 3))
            def _():
                pick(0)

            @pl.when(t == 3)
            def _():
                gathered(j + 1)

            last = t == 3
            j_next = jnp.where(last, j + 1, j)
            pair(j, 2 * t, 2 * t + 1, j_next, jnp.where(last, 2 * j + 2, 2 * t + 2))
            return 0

        lax.fori_loop(j + 1, 4, inner, 0)
        return 0

    gathered(0)
    s0[...] = scores(0, 0)
    lax.fori_loop(0, 4, stretch_run, 0)

    def last_tile(n):
        step = jnp.int32(LAST[7])
        for m in range(7):
            step = jnp.where(n % 8 == m, LAST[m], step)
        return turned(step)

    def chunk_run(c, _):
        @pl.when(c == 5)
        def _():
            forward_prefix(1, 0)

        def inner(t, _):
            @pl.when((c == 4) & (t == 2))
            def _():
                forward_prefix(0, 0)
                forward_prefix(0, 1)

            @pl.when((c == 5) & (t == 3))
            def _():
                forward_prefix(1, 1)

            last = t == 3
            a_next = jnp.where(last & (c == 5), last_tile(0), (2 * t + 2) % 8)
            pair(c, 2 * t, 2 * t + 1, jnp.where(last, c + 1, c), a_next)
            return 0

        lax.fori_loop(0, 4, inner, 0)
        return 0

    lax.fori_loop(4, 6, chunk_run, 0)
    for n in range(2):
        for u in range(2):
            prefix_on(n, u).wait_recv()

    mine = pl.ds(pl.multiple_of(h * 512, 512), 512)

    def out_copy(i):
        return remote(ob.at[i], o_ref.at[:, mine], s_o.at[i], r_o.at[h], (g, i * 4 + z))

    def own_copy(i):
        return pltpu.make_async_copy(ob.at[i], o_ref.at[:, mine], s_o.at[i])

    def finish(i):
        total = acc[i]
        out = total[0:128] / total[128:129]
        for m in range(4):
            lanes = slice(m * 128, (m + 1) * 128)
            ob[i, :, lanes] = out[:, lanes].T.astype(BF)

        @pl.when(i != h)
        def _():
            out_copy(i).start()

        @pl.when(i == h)
        def _():
            own_copy(i).start()

    def last_run(n, _):
        i = last_tile(n)
        pen = [[pens[c, m] for m in range(8)] for c in (6, 7)]
        s1[...] = scores(7, i)
        soften(s0, 6, i, 8, pen[0])
        s0[...] = scores(6, last_tile(n + 1))
        soften(s1, 7, i, 8, pen[1])
        finish(i)
        return 0

    lax.fori_loop(0, 8, last_run, 0)

    sib_copy.wait_send()
    for copy in st_copies + q_copies + p_copies[0] + p_copies[1]:
        copy.wait_send()
    for j in range(4):
        for copy in (stretch_up(j), stretch_down(j), stretch_on_up(j), stretch_on_down(j)):
            copy.wait_send()
    for n in range(2):
        for u in range(2):
            for copy in (prefix_up(n, u), prefix_down(n, u), prefix_on(n, u)):
                copy.wait_send()

    def settle(i, _):
        @pl.when(i != h)
        def _():
            out_copy(i).wait_send()
            lanes = pl.ds(pl.multiple_of(i * 512, 512), 512)
            remote(ob.at[i], o_ref.at[:, lanes], s_o.at[i], r_o.at[i], (g, i * 4 + z)).wait_recv()

        @pl.when(i == h)
        def _():
            own_copy(i).wait()

        return 0

    lax.fori_loop(0, 8, settle, 0)


def local(queries, keys, values, cache_k, cache_v, holder, prefix_len):
    hbm = pl.BlockSpec(memory_space=pl.ANY)
    smem = pl.BlockSpec(memory_space=pltpu.SMEM)
    dma = pltpu.SemaphoreType.DMA
    out = pl.pallas_call(
        attend_kernel,
        out_shape=pltpu.VMEM((128, 4096), BF),
        in_specs=[hbm] * 5 + [smem, smem],
        out_specs=pl.BlockSpec(memory_space=pltpu.VMEM),
        scratch_shapes=[
            pltpu.VMEM((8, 2, 4, 2, 128, 128), BF),
            pltpu.VMEM((8, 128, 512), BF),
            pltpu.VMEM((8, 144, 512), F32),
            pltpu.VMEM((8, 1, 512), F32),
            pltpu.VMEM((1024, 512), F32),
            pltpu.VMEM((1024, 512), F32),
            pltpu.VMEM((8, 128, 512), BF),
            pltpu.VMEM((8, 2, 128, 128), BF),
            pltpu.VMEM((2, 2, 128, 1024), BF),
            pltpu.VMEM((2, 2, 128, 1024), BF),
            pltpu.VMEM((2, 2, 8, 128, 128), BF),
            pltpu.VMEM((2, 8, 128, 128), BF),
            pltpu.VMEM((2, 8, 128, 128), BF),
            pltpu.VMEM((128, 1024), BF),
            pltpu.VMEM((128, 1024), BF),
            pltpu.VMEM((2, 128, 1024), BF),
            pltpu.VMEM((2, 128, 1024), BF),
            pltpu.SMEM((8, 8), F32),
            dma((5,)),
            dma((1,)), dma((1,)),
            dma((8,)), dma((8,)),
            dma((8,)), dma((8,)),
            dma((2, 16)), dma((2, 16)),
            dma((4, 2)), dma((4, 2)),
            dma((4, 2)), dma((4, 2)),
            dma((2, 2, 2)), dma((2, 2, 2)),
            dma((2, 2)), dma((2, 2)),
            dma((8,)), dma((8,)),
        ],
        compiler_params=pltpu.CompilerParams(
            collective_id=0, has_side_effects=True, vmem_limit_bytes=56 * 2**20
        ),
        cost_estimate=pl.CostEstimate(flops=14 * 10**9, bytes_accessed=4 * 2**20, transcendentals=27 * 10**6),
        name="attend",
    )(
        queries[0], keys[0], values[0], cache_k[0, 0], cache_v[0, 0], holder[:, :, 0].T, prefix_len,
    )
    return out[None]


def solution(mesh):
    return jax.shard_map(
        local,
        mesh=mesh,
        in_specs=(
            P("grp", "blk", None),
            P("grp", "blk", None),
            P("grp", "blk", None),
            P("grp", "blk", None, None, None),
            P("grp", "blk", None, None, None),
            P(),
            P(),
        ),
        out_specs=P("grp", "blk", None),
        check_vma=False,
    )
```

```python
import functools

import jax
import jax.numpy as jnp
from jax import lax
from jax.experimental import pallas as pl
from jax.experimental.pallas import tpu as pltpu
from jax.sharding import PartitionSpec as P

MESH = pl.DeviceIdType.MESH
BF = jnp.bfloat16
F32 = jnp.float32
BIG = 1e30
SCALE = 1.4426950408889634 / (128.0 ** 0.5)
ORDER = (4, 1, 3, 5, 7, 6, 2)
LAST = (6, 2, 5, 7, 4, 1, 3, 0)


def attend_kernel(
    q_ref, k_ref, v_ref, ck_ref, cv_ref, holder_ref, plen_ref, o_ref,
    kv, q_in, acc, top, s0, s1, ob,
    skv, sib_out, sib_in, cand, pc_k, pc_v, k_in, v_in, ck_in, cv_in, pens,
    s_in, s_sib, r_sib, s_st, r_st, s_q, r_q, s_p, r_p, s_z, r_z, s_f, r_f, s_zp, r_zp, s_fp, r_fp, s_o, r_o,
):
    g = lax.axis_index("grp")
    b = lax.axis_index("blk")
    xh, core = g // 2, g % 2
    h, z = b // 4, b % 4

    def turned(d):
        return ((h // 4 + d // 4) % 2) * 4 + (h % 4 + d % 4) % 4

    def plane(d):
        return (g, turned(d) * 4 + z)

    def across(d):
        return ((1 - xh) * 2 + core, turned(d) * 4 + z)

    sibling = (xh * 2 + 1 - core, b)
    z_up = (g, h * 4 + (z + 1) % 4)
    z_down = (g, h * 4 + (z + 3) % 4)

    barrier = pltpu.get_barrier_semaphore()
    peers = [plane(d) for d in range(1, 8)] + [across(d) for d in range(8)] + [sibling, z_up, z_down]
    for peer in peers:
        pl.semaphore_signal(barrier, inc=1, device_id=peer, device_id_type=MESH)

    def remote(src, dst, send, recv, peer):
        return pltpu.make_async_remote_copy(
            src_ref=src, dst_ref=dst, send_sem=send, recv_sem=recv, device_id=peer, device_id_type=MESH
        )

    def held(c):
        own = holder_ref[c, b]
        slot = jnp.int32(0)
        for c2 in range(4):
            slot = slot + jnp.where((c2 < c) & (holder_ref[c2, b] == own), 1, 0)
        return own, jnp.minimum(slot, 1)

    fetches = [
        pltpu.make_async_copy(src, dst, s_in.at[n])
        for n, (src, dst) in enumerate(((k_ref, k_in), (v_ref, v_in), (ck_ref, ck_in), (cv_ref, cv_in)))
    ]
    for fetch in fetches:
        fetch.start()
    own_queries = pltpu.make_async_copy(
        q_ref.at[:, pl.ds(pl.multiple_of(h * 512, 512), 512)], q_in.at[h], s_in.at[4]
    )
    own_queries.start()
    fetches[0].wait()
    fetches[1].wait()
    for p in range(8):
        lanes = slice(p * 128, (p + 1) * 128)
        skv[p, 0] = k_in[:, lanes]
        skv[p, 1] = v_in[:, lanes].T

    pl.semaphore_wait(barrier, len(peers))

    st_copies, q_copies, p_copies = [], [], ([], [])
    for d in ORDER:
        to = turned(d)
        copy = remote(skv.at[to], kv.at[h // 2, h % 2, 0], s_st.at[d], r_st.at[d], plane(d))
        copy.start()
        st_copies.append(copy)
    for d in ORDER:
        to = turned(d)
        lanes = pl.ds(pl.multiple_of(to * 512, 512), 512)
        copy = remote(q_ref.at[:, lanes], q_in.at[h], s_q.at[d], r_q.at[d], plane(d))
        copy.start()
        q_copies.append(copy)

    fetches[2].wait()
    fetches[3].wait()
    for e in range(2):
        _, slot = held(2 * e + 1 - core)
        sib_out[e, 0] = ck_in[slot]
        sib_out[e, 1] = cv_in[slot]
    sib_copy = remote(sib_out, sib_in, s_sib.at[0], r_sib.at[0], sibling)
    sib_copy.start()
    kv[h // 2, h % 2, 0] = skv[h]
    plen = plen_ref[g]
    for c in range(4, 8):
        for n in range(8):
            if c in (4, 7):
                block = 4 * n + (z + 2 * (c // 7)) % 4
            else:
                block = 4 * (4 * (c - 5) + n % 4) + (z + 3 - 2 * (n // 4)) % 4
            pens[c, n] = jnp.where(block < plen, 0.0, BIG)
    for c in range(4):
        for n in range(8):
            pens[c, n] = 0.0
    top[...] = jnp.full(top.shape, -BIG, F32)
    acc[...] = jnp.zeros(acc.shape, F32)

    def send_prefix(n, cache):
        for e in range(2):
            own, slot = held(2 * e + core)
            from_sibling = own == xh * 2 + 1 - core
            for p in range(8):
                lanes = slice(p * 128, (p + 1) * 128)
                part = jnp.where(from_sibling, sib_in[e, n, :, lanes], cache[slot, :, lanes])
                cand[n, e, p] = part.T if n else part
        for d in (0,) + ORDER:
            to = turned(d)
            copy = remote(cand.at[n, 1 - xh, to], (pc_k, pc_v)[n].at[xh, h], s_p.at[n, 8 + d], r_p.at[n, 8 + d], across(d))
            copy.start()
            p_copies[n].append(copy)
            if d:
                copy = remote(cand.at[n, xh, to], (pc_k, pc_v)[n].at[xh, h], s_p.at[n, d], r_p.at[n, d], plane(d))
                copy.start()
                p_copies[n].append(copy)
        (pc_k, pc_v)[n][xh, h] = cand[n, xh, h]

    def stretch_up(j):
        return remote(kv.at[j, :, 0], kv.at[j, :, 1], s_z.at[j, 0], r_z.at[j, 0], z_up)

    def stretch_down(j):
        return remote(kv.at[j, :, 0], kv.at[j, :, 3], s_z.at[j, 1], r_z.at[j, 1], z_down)

    def stretch_on_up(j):
        return remote(kv.at[j, :, 1, 0], kv.at[j, :, 2, 0], s_f.at[j, 0], r_f.at[j, 0], z_up)

    def stretch_on_down(j):
        return remote(kv.at[j, :, 3, 1], kv.at[j, :, 2, 1], s_f.at[j, 1], r_f.at[j, 1], z_down)

    def prefix_up(n, u):
        return remote(kv.at[4, u, :, n], kv.at[5 + u, 0, :, n], s_zp.at[n, u, 0], r_zp.at[n, u, 0], z_up)

    def prefix_down(n, u):
        return remote(kv.at[4, u, :, n], kv.at[5 + u, 1, :, n], s_zp.at[n, u, 1], r_zp.at[n, u, 1], z_down)

    def prefix_on(n, u):
        return remote(kv.at[5 + u, u, :, n], kv.at[7, u, :, n], s_fp.at[n, u], r_fp.at[n, u], (z_up, z_down)[u])

    def forward_prefix(n, u):
        here, other = (prefix_up, prefix_down) if u == 0 else (prefix_down, prefix_up)
        here(n, u).wait_recv()
        prefix_on(n, u).start()
        other(n, u).wait_recv()

    def send_stretch(j):
        stretch_up(j).start()
        stretch_down(j).start()

    def forward_stretch(j):
        stretch_up(j).wait_recv()
        stretch_on_up(j).start()
        stretch_down(j).wait_recv()
        stretch_on_down(j).start()

    def pick(n):
        for copy in p_copies[n]:
            copy.wait_recv()
        for i in range(8):
            side = holder_ref[g, 4 * i + z] // 2
            kv[4, i // 4, i % 4, n] = (pc_k, pc_v)[n][side, i]
        for u in range(2):
            prefix_up(n, u).start()
            prefix_down(n, u).start()

    sib_copy.wait_recv()
    send_prefix(0, ck_in)
    for copy in st_copies:
        copy.wait_recv()
    send_stretch(0)
    send_stretch(1)
    send_prefix(1, cv_in)
    for j in range(3):
        forward_stretch(j)
        if j < 2:
            send_stretch(j + 2)

    for copy in q_copies:
        copy.wait_recv()
    own_queries.wait()

    def scores(c, i):
        keys = kv[c, :, :, 0].reshape(1024, 128)
        queries = jnp.concatenate([q_in[i, :, m * 128 : (m + 1) * 128] for m in range(4)], axis=0)
        return lax.dot_general(keys, queries, (((1,), (1,)), ((), ())), preferred_element_type=F32)

    def soften(s_ref, c, i, blocks, pen, corner=None):
        parts = []
        best = top[i]
        for n in range(blocks):
            part = s_ref[n * 128 : (n + 1) * 128, :]
            if n == corner:
                key_at = lax.broadcasted_iota(jnp.int32, (128, 512), 0)
                query_at = lax.broadcasted_iota(jnp.int32, (128, 512), 1) % 128
                part = jnp.where(key_at <= query_at, part, -BIG)
            parts.append(part)
            high = jnp.max(part, axis=0, keepdims=True)
            if pen[n] is not None:
                high = high - pen[n]
            best = jnp.maximum(best, high)
        fade = jnp.exp2((top[i] - best) * SCALE)
        top[i] = best
        weights = []
        for n in range(blocks):
            base = best if pen[n] is None else best + pen[n]
            weights.append(jnp.exp2((parts[n] - base) * SCALE).astype(BF))
        weights = jnp.concatenate(weights, axis=0)
        values_t = jnp.concatenate([kv[c, n // 4, n % 4, 1] for n in range(blocks)], axis=1)
        values_t = jnp.concatenate([values_t, jnp.ones((16, blocks * 128), BF)], axis=0)
        acc[i] = acc[i] * fade + jnp.dot(values_t, weights, preferred_element_type=F32)

    def pair(c, a, b, c_next, a_next):
        pen = [pens[c, n] for n in range(8)]
        s1[...] = scores(c, b)
        soften(s0, c, a, 8, pen)
        s0[...] = scores(c_next, a_next)
        soften(s1, c, b, 8, pen)

    later = [jnp.where(r <= z, 0.0, BIG) for r in range(4)]

    def diagonal(t):
        s1[...] = scores(t, 2 * t + 1)
        soften(s0, t, 2 * t, 4, [None] + later[1:], corner=0)
        s0[...] = scores(jnp.where(t == 3, 4, t), (2 * t + 2) % 8)
        soften(s1, t, 2 * t + 1, 8, [None] * 5 + later[1:], corner=4)

    def gathered(j):
        stretch_on_up(j).wait_recv()
        stretch_on_down(j).wait_recv()

    def stretch_run(j, _):
        diagonal(j)

        def inner(t, _):
            @pl.when((j == 0) & (t == 2))
            def _():
                forward_stretch(3)

            @pl.when((j == 2) & (t == 3))
            def _():
                pick(1)

            @pl.when((j == 0) & (t == 3))
            def _():
                pick(0)

            @pl.when(t == 3)
            def _():
                gathered(j + 1)

            last = t == 3
            j_next = jnp.where(last, j + 1, j)
            pair(j, 2 * t, 2 * t + 1, j_next, jnp.where(last, 2 * j + 2, 2 * t + 2))
            return 0

        lax.fori_loop(j + 1, 4, inner, 0)
        return 0

    gathered(0)
    s0[...] = scores(0, 0)
    lax.fori_loop(0, 4, stretch_run, 0)

    def last_tile(n):
        step = jnp.int32(LAST[7])
        for m in range(7):
            step = jnp.where(n % 8 == m, LAST[m], step)
        return turned(step)

    def chunk_run(c, _):
        @pl.when(c == 5)
        def _():
            forward_prefix(1, 0)

        def inner(t, _):
            @pl.when((c == 4) & (t == 2))
            def _():
                forward_prefix(0, 0)
                forward_prefix(0, 1)

            @pl.when((c == 5) & (t == 3))
            def _():
                forward_prefix(1, 1)

            last = t == 3
            a_next = jnp.where(last & (c == 5), last_tile(0), (2 * t + 2) % 8)
            pair(c, 2 * t, 2 * t + 1, jnp.where(last, c + 1, c), a_next)
            return 0

        lax.fori_loop(0, 4, inner, 0)
        return 0

    lax.fori_loop(4, 6, chunk_run, 0)
    for n in range(2):
        for u in range(2):
            prefix_on(n, u).wait_recv()

    mine = pl.ds(pl.multiple_of(h * 512, 512), 512)

    def out_copy(i):
        return remote(ob.at[i], o_ref.at[:, mine], s_o.at[i], r_o.at[h], (g, i * 4 + z))

    def own_copy(i):
        return pltpu.make_async_copy(ob.at[i], o_ref.at[:, mine], s_o.at[i])

    def finish(i):
        total = acc[i]
        out = total[0:128] / total[128:129]
        for m in range(4):
            lanes = slice(m * 128, (m + 1) * 128)
            ob[i, :, lanes] = out[:, lanes].T.astype(BF)

        @pl.when(i != h)
        def _():
            out_copy(i).start()

        @pl.when(i == h)
        def _():
            own_copy(i).start()

    def last_run(n, _):
        i = last_tile(n)
        pen = [[pens[c, m] for m in range(8)] for c in (6, 7)]
        s1[...] = scores(7, i)
        soften(s0, 6, i, 8, pen[0])
        s0[...] = scores(6, last_tile(n + 1))
        soften(s1, 7, i, 8, pen[1])
        finish(i)
        return 0

    lax.fori_loop(0, 8, last_run, 0)

    sib_copy.wait_send()
    for copy in st_copies + q_copies + p_copies[0] + p_copies[1]:
        copy.wait_send()
    for j in range(4):
        for copy in (stretch_up(j), stretch_down(j), stretch_on_up(j), stretch_on_down(j)):
            copy.wait_send()
    for n in range(2):
        for u in range(2):
            for copy in (prefix_up(n, u), prefix_down(n, u), prefix_on(n, u)):
                copy.wait_send()

    def settle(i, _):
        @pl.when(i != h)
        def _():
            out_copy(i).wait_send()
            lanes = pl.ds(pl.multiple_of(i * 512, 512), 512)
            remote(ob.at[i], o_ref.at[:, lanes], s_o.at[i], r_o.at[i], (g, i * 4 + z)).wait_recv()

        @pl.when(i == h)
        def _():
            own_copy(i).wait()

        return 0

    lax.fori_loop(0, 8, settle, 0)


def local(queries, keys, values, cache_k, cache_v, holder, prefix_len):
    hbm = pl.BlockSpec(memory_space=pl.ANY)
    smem = pl.BlockSpec(memory_space=pltpu.SMEM)
    dma = pltpu.SemaphoreType.DMA
    out = pl.pallas_call(
        attend_kernel,
        out_shape=pltpu.VMEM((128, 4096), BF),
        in_specs=[hbm] * 5 + [smem, smem],
        out_specs=pl.BlockSpec(memory_space=pltpu.VMEM),
        scratch_shapes=[
            pltpu.VMEM((8, 2, 4, 2, 128, 128), BF),
            pltpu.VMEM((8, 128, 512), BF),
            pltpu.VMEM((8, 144, 512), F32),
            pltpu.VMEM((8, 1, 512), F32),
            pltpu.VMEM((1024, 512), F32),
            pltpu.VMEM((1024, 512), F32),
            pltpu.VMEM((8, 128, 512), BF),
            pltpu.VMEM((8, 2, 128, 128), BF),
            pltpu.VMEM((2, 2, 128, 1024), BF),
            pltpu.VMEM((2, 2, 128, 1024), BF),
            pltpu.VMEM((2, 2, 8, 128, 128), BF),
            pltpu.VMEM((2, 8, 128, 128), BF),
            pltpu.VMEM((2, 8, 128, 128), BF),
            pltpu.VMEM((128, 1024), BF),
            pltpu.VMEM((128, 1024), BF),
            pltpu.VMEM((2, 128, 1024), BF),
            pltpu.VMEM((2, 128, 1024), BF),
            pltpu.SMEM((8, 8), F32),
            dma((5,)),
            dma((1,)), dma((1,)),
            dma((8,)), dma((8,)),
            dma((8,)), dma((8,)),
            dma((2, 16)), dma((2, 16)),
            dma((4, 2)), dma((4, 2)),
            dma((4, 2)), dma((4, 2)),
            dma((2, 2, 2)), dma((2, 2, 2)),
            dma((2, 2)), dma((2, 2)),
            dma((8,)), dma((8,)),
        ],
        compiler_params=pltpu.CompilerParams(
            collective_id=0, has_side_effects=True, vmem_limit_bytes=56 * 2**20
        ),
        cost_estimate=pl.CostEstimate(flops=14 * 10**9, bytes_accessed=4 * 2**20, transcendentals=27 * 10**6),
        name="attend",
    )(
        queries[0], keys[0], values[0], cache_k[0, 0], cache_v[0, 0], holder[:, :, 0].T, prefix_len,
    )
    return out[None]


def solution(mesh):
    return jax.shard_map(
        local,
        mesh=mesh,
        in_specs=(
            P("grp", "blk", None),
            P("grp", "blk", None),
            P("grp", "blk", None),
            P("grp", "blk", None, None, None),
            P("grp", "blk", None, None, None),
            P(),
            P(),
        ),
        out_specs=P("grp", "blk", None),
        check_vma=False,
    )
```
